32 devices in a mesh: fsdp: 32 (over z, y, x, core), tp: 1.
Axes of the slice: x: 2, y: 2, z: 4, core: 2. Of those that a mesh axis runs over, the one named last changes fastest.
Arguments:
- hidden_in: bfloat16 [32768, 5120], P('fsdp', 'tp'), may hold values from -6 to 6
- out_grad: bfloat16 [32768, 5120], P('fsdp', 'tp'), may hold values from -36 to 36
- rewards: float32 [64], P('fsdp'), may hold values from -5 to 5
- group_ids: int32 [64], replicated, may hold values from 0 to 7, as said below
- weight: bfloat16 [5120, 5120], P('fsdp', 'tp'), may hold values from -0.078125 to 0.078125
- adam_m: float32 [5120, 5120], P('fsdp', 'tp'), may hold values from -6 to 6
- adam_v: float32 [5120, 5120], P('fsdp', 'tp'), may hold values from 0.05 to 2
- given_queries: bfloat16 [512, 4, 5120], P('fsdp', None, 'tp'), may hold values from -24 to 24
- given_keys: bfloat16 [512, 4, 1024], P('fsdp', None, 'tp'), may hold values from -4 to 4
- given_values: bfloat16 [512, 4, 1024], P('fsdp', None, 'tp'), may hold values from -12 to 12
- stored_keys: bfloat16 [512, 8, 512, 128], P('fsdp', 'tp'), may hold values from -24 to 24
- stored_values: bfloat16 [512, 8, 512, 128], P('fsdp', 'tp'), may hold values from -12 to 12
- cache_fill_length: int32 [512], P('fsdp'), may hold values from 128 to 508
Outputs:
- new_weight: bfloat16 [5120, 5120], P('fsdp', 'tp')
- new_m: float32 [5120, 5120], P('fsdp', 'tp')
- new_v: float32 [5120, 5120], P('fsdp', 'tp')
- layer_out: float32 [512, 4, 5120], P('fsdp', None, 'tp')
The draws below stay inside these ranges and needn't reach their ends.
Inputs may be any that keep to these rules, and one draw needn't show every extreme that they name: `group_ids`: each group number names exactly 8 sequences.
All inputs are finite; a program needn't handle non-finite values.
Results may differ from the reference program's by a relative error of at most 0.0059.
Values may be sent and summed in bfloat16 or wider, within the bound.
A program may use at most 384 MiB of HBM per device.

```python
import math
import jax
import jax.numpy as jnp
from jax import lax

D = 5120
QUERY_HEADS = 40
KEY_VALUE_HEADS = 8
HEAD_SIZE = 128
QUERY_FEATURES = 5120
SEQ_LEN = 512
TOK_DEV = 1024
SEQS = 64
TOKENS = 32768
GSIZE = 8
GROUPS = 8
REPLICA_ROWS = 16
TOTAL_ROWS = 512
CACHE_SLOTS = 512
GIVEN_TOKENS = 4
OPT_STEP = 10
N_FSDP = 32


def draw_stored_keys(key, part):
    key = jax.random.fold_in(key, 1)
    value_rows = jnp.clip(jax.random.normal(key, (TOTAL_ROWS, KEY_VALUE_HEADS, CACHE_SLOTS, HEAD_SIZE), jnp.float32), -4.0, 4.0)
    return value_rows.astype(jnp.bfloat16)


def draw_given_queries(key, part):
    key = jax.random.fold_in(key, 2)
    value_rows = jnp.clip(jax.random.normal(key, (TOTAL_ROWS, GIVEN_TOKENS, QUERY_HEADS * HEAD_SIZE), jnp.float32), -4.0, 4.0)
    return value_rows.astype(jnp.bfloat16)


def draw_cache_fill_length(key, part):
    key = jax.random.fold_in(key, 3)
    lengths = jax.random.randint(key, (TOTAL_ROWS,), CACHE_SLOTS // 4, CACHE_SLOTS - GIVEN_TOKENS + 1, dtype=jnp.int32)
    lengths = lengths.at[0].set(CACHE_SLOTS - GIVEN_TOKENS)
    lengths = lengths.at[1].set(CACHE_SLOTS // 4)
    return lengths


def draw_group_ids(key, part):
    key = jax.random.fold_in(key, 4)
    order = jax.random.permutation(key, SEQS)
    return (order // GSIZE).astype(jnp.int32)


def strengthened(drawn, rng, source, target, blocks, factor):
    def block_of(dim):
        return (jnp.arange(drawn.shape[dim]) // (drawn.shape[dim] // blocks)).reshape((-1,) + (1,) * (drawn.ndim - 1 - dim))

    one_side = jax.random.permutation(rng, blocks)[block_of(target)]
    other_side = (block_of(target) + blocks // 2) % blocks
    return jnp.where((block_of(source) == one_side) | (block_of(source) == other_side), factor * drawn, drawn)


def shard_levels(key, dims, shards, low, high):
    level, own = 1.0, jax.random.fold_in(key, 6)
    for axis_at, shards_of in shards:
        draws = jnp.exp(jax.random.uniform(jax.random.fold_in(own, axis_at), (shards_of,), jnp.float32, low / len(shards), high / len(shards)))
        level = level * jnp.repeat(draws, dims[axis_at] // shards_of).reshape([-1 if axis == axis_at else 1 for axis in range(len(dims))])
    return level


def centred(own_key, dims, scale, limit, cuts=(), kind=jnp.bfloat16):
    level = shard_levels(own_key, dims, cuts, -0.22, 0.18) if cuts else 1.0
    array = jax.random.normal(own_key, dims, jnp.float32) * scale * level
    return jnp.minimum(jnp.maximum(array, -limit), limit).astype(kind)


def noise_with(stream_key, extent, scale, bound, cuts, heavy, kind=jnp.bfloat16):
    values = scale * jax.random.normal(stream_key, extent, jnp.float32)
    if cuts:
        values = values * shard_levels(stream_key, extent, cuts, -0.22, 0.18)
    return jnp.clip(strengthened(values, jax.random.fold_in(stream_key, 3), *heavy), -bound, bound).astype(kind)


def setup_inputs(seed: int = 0) -> dict:
    key_list = jax.random.split(jax.random.key(seed), 14)
    return {
        "hidden_in": centred(key_list[0], (TOKENS, QUERY_FEATURES), 1.0, 6.0, ((0, 32),)),
        "out_grad": noise_with(key_list[1], (TOKENS, D), 6.0, 36.0, ((0, 32),), (0, 1, 32, 2.75)),
        "rewards": centred(key_list[2], (SEQS,), 1.0, 5.0, ((0, 32),), jnp.float32),
        "group_ids": draw_group_ids(jax.random.fold_in(key_list[13], 71), 0),
        "weight": centred(key_list[4], (D, QUERY_FEATURES), QUERY_FEATURES ** -0.5, 0.078125, ((0, 32),)),
        "adam_m": centred(key_list[5], (D, QUERY_FEATURES), 1.0, 6.0, ((0, 32),), jnp.float32),
        "adam_v": jnp.clip(jnp.exp(math.log(2.0) - 3.6888794 * jax.random.uniform(key_list[6], (D, QUERY_FEATURES), jnp.float32) ** shard_levels(key_list[6], (D, QUERY_FEATURES), ((0, 32),), -0.2, 0.2)), 0.05, 2.0),
        "given_queries": draw_given_queries(jax.random.fold_in(key_list[13], 71), 0),
        "given_keys": centred(key_list[8], (TOTAL_ROWS, GIVEN_TOKENS, KEY_VALUE_HEADS * HEAD_SIZE), 1.0, 4.0, ((0, 32),)),
        "given_values": centred(key_list[9], (TOTAL_ROWS, GIVEN_TOKENS, KEY_VALUE_HEADS * HEAD_SIZE), 3.0, 12.0, ((0, 32),)),
        "stored_keys": draw_stored_keys(jax.random.fold_in(key_list[13], 71), 0),
        "stored_values": centred(key_list[11], (TOTAL_ROWS, KEY_VALUE_HEADS, CACHE_SLOTS, HEAD_SIZE), 3.0, 12.0, ((0, 32),)),
        "cache_fill_length": draw_cache_fill_length(jax.random.fold_in(key_list[13], 71), 0),
    }


beta_one = 0.9
beta_two = 0.95
adam_eps = 1e-08
learn_rate = 0.002
decay_rate = 0.1
std_floor = 0.75

def group_advantage(rewards, group_ids):
    labels = jnp.arange(GROUPS, dtype=jnp.int32)
    member = (group_ids[:, None] == labels[None, :]).astype(jnp.float32)
    group_mean = lax.optimization_barrier(jnp.sum(member * rewards[:, None], axis=0)) / GSIZE
    spread = rewards - lax.optimization_barrier(jnp.sum(member * group_mean[None, :], axis=1))
    group_var = lax.optimization_barrier(jnp.sum(member * (spread * spread)[:, None], axis=0)) / (GSIZE - 1)
    own_std = jnp.sqrt(lax.optimization_barrier(jnp.sum(member * group_var[None, :], axis=1)))
    return spread / jnp.maximum(own_std, std_floor)

def attend_block(query_in, key_new, value_new, key_cache, value_cache, lengths):
    row_count = query_in.shape[0]
    step_count = query_in.shape[1]
    kv_heads = key_cache.shape[1]
    cache_size = key_cache.shape[2]
    head_dim = key_cache.shape[3]
    group_size = query_in.shape[2] // (kv_heads * head_dim)
    scaling = 1.0 / math.sqrt(head_dim)
    query_heads = query_in.reshape(row_count, step_count, kv_heads, group_size, head_dim).astype(jnp.float32)
    fresh_keys = key_new.reshape(row_count, step_count, kv_heads, head_dim).astype(jnp.float32)
    fresh_values = value_new.reshape(row_count, step_count, kv_heads, head_dim).astype(jnp.float32)
    cache_score = jnp.einsum('rsKgd,rKcd->rKgsc', query_heads, key_cache.astype(jnp.float32)) * scaling
    fresh_score = jnp.einsum('rsKgd,rtKd->rKgst', query_heads, fresh_keys) * scaling
    cache_mask = jnp.arange(cache_size, dtype=jnp.int32)[None, :] < lengths[:, None]
    step_index = jnp.arange(step_count, dtype=jnp.int32)
    fresh_mask = step_index[None, :] <= step_index[:, None]
    cache_score = jnp.where(cache_mask[:, None, None, None, :], cache_score, -jnp.inf)
    fresh_score = jnp.where(fresh_mask, fresh_score, -jnp.inf)
    peak_score = jnp.maximum(lax.optimization_barrier(jnp.max(cache_score, axis=-1, keepdims=True)), lax.optimization_barrier(jnp.max(fresh_score, axis=-1, keepdims=True)))
    cache_exp = jnp.exp(cache_score - peak_score)
    fresh_exp = jnp.exp(fresh_score - peak_score)
    total_exp = lax.optimization_barrier(jnp.sum(cache_exp, axis=-1, keepdims=True)) + lax.optimization_barrier(jnp.sum(fresh_exp, axis=-1, keepdims=True))
    cache_prob = (cache_exp / total_exp).astype(jnp.bfloat16)
    fresh_prob = (fresh_exp / total_exp).astype(jnp.bfloat16)
    mixed = jnp.einsum('rKgsc,rKcd->rsKgd', cache_prob.astype(jnp.float32), value_cache.astype(jnp.float32))
    mixed = mixed + jnp.einsum('rKgst,rtKd->rsKgd', fresh_prob.astype(jnp.float32), fresh_values)
    return mixed.reshape(row_count, step_count, kv_heads * group_size * head_dim).astype(jnp.bfloat16)

def reference(hidden_in, out_grad, rewards, group_ids, weight, adam_m, adam_v, given_queries, given_keys, given_values, stored_keys, stored_values, cache_fill_length):
    advantage = group_advantage(rewards, group_ids)
    token_adv = jnp.repeat(advantage, SEQ_LEN)
    weighted = (hidden_in.astype(jnp.float32) * token_adv[:, None] / SEQS).astype(jnp.bfloat16)

    def accumulate(total, index):
        start = (index * TOK_DEV).astype(jnp.int32)
        cot_rows = lax.dynamic_slice_in_dim(out_grad, start, TOK_DEV, 0).astype(jnp.float32)
        act_rows = lax.dynamic_slice_in_dim(weighted, start, TOK_DEV, 0).astype(jnp.float32)
        partial_sum = jnp.dot(cot_rows.T, act_rows, preferred_element_type=jnp.float32)
        return (total + partial_sum, None)
    gradient, _ = lax.scan(accumulate, jnp.zeros((D, QUERY_FEATURES), jnp.float32), jnp.arange(N_FSDP, dtype=jnp.int32))
    new_m = beta_one * adam_m + (1.0 - beta_one) * gradient
    new_v = beta_two * adam_v + (1.0 - beta_two) * gradient * gradient
    correct_one = 1.0 - beta_one ** OPT_STEP
    correct_two = 1.0 - beta_two ** OPT_STEP
    update = new_m / correct_one / (jnp.sqrt(new_v / correct_two) + adam_eps)
    new_weight = (weight.astype(jnp.float32) * (1.0 - learn_rate * decay_rate) - learn_rate * update).astype(jnp.bfloat16)

    def replica(inputs):
        return attend_block(*inputs)
    block_list = (given_queries.reshape(N_FSDP, REPLICA_ROWS, GIVEN_TOKENS, QUERY_FEATURES), given_keys.reshape(N_FSDP, REPLICA_ROWS, GIVEN_TOKENS, KEY_VALUE_HEADS * HEAD_SIZE), given_values.reshape(N_FSDP, REPLICA_ROWS, GIVEN_TOKENS, KEY_VALUE_HEADS * HEAD_SIZE), stored_keys.reshape(N_FSDP, REPLICA_ROWS, KEY_VALUE_HEADS, CACHE_SLOTS, HEAD_SIZE), stored_values.reshape(N_FSDP, REPLICA_ROWS, KEY_VALUE_HEADS, CACHE_SLOTS, HEAD_SIZE), cache_fill_length.reshape(N_FSDP, REPLICA_ROWS))
    attn = lax.map(replica, block_list).reshape(TOTAL_ROWS * GIVEN_TOKENS, QUERY_FEATURES)
    projected = jnp.dot(attn.astype(jnp.float32), new_weight.astype(jnp.float32).T, preferred_element_type=jnp.float32)
    layer_out = projected.reshape(TOTAL_ROWS, GIVEN_TOKENS, D)
    return (new_weight, new_m, new_v, layer_out)
```

```python
import math

import jax
import jax.numpy as jnp
from jax import lax
from jax.sharding import PartitionSpec as P

GSIZE = 8
OPT_STEP = 10


beta_one = 0.9
beta_two = 0.95
adam_eps = 1e-08
learn_rate = 0.002
decay_rate = 0.1
std_floor = 0.75


def attend_local(query_in, key_new, value_new, key_cache, value_cache, lengths):
    row_count = query_in.shape[0]
    step_count = query_in.shape[1]
    kv_heads = key_cache.shape[1]
    cache_size = key_cache.shape[2]
    head_dim = key_cache.shape[3]
    group_size = query_in.shape[2] // (kv_heads * head_dim)
    scaling = 1.0 / math.sqrt(head_dim)
    query_heads = query_in.reshape(row_count, step_count, kv_heads, group_size, head_dim)
    fresh_keys = key_new.reshape(row_count, step_count, kv_heads, head_dim)
    fresh_values = value_new.reshape(row_count, step_count, kv_heads, head_dim)
    cache_score = (
        jnp.einsum("rsKgd,rKcd->rKgsc", query_heads, key_cache, preferred_element_type=jnp.float32)
        * scaling
    )
    fresh_score = (
        jnp.einsum("rsKgd,rtKd->rKgst", query_heads, fresh_keys, preferred_element_type=jnp.float32)
        * scaling
    )
    cache_mask = jnp.arange(cache_size, dtype=jnp.int32)[None, :] < lengths[:, None]
    step_index = jnp.arange(step_count, dtype=jnp.int32)
    fresh_mask = step_index[None, :] <= step_index[:, None]
    cache_score = jnp.where(cache_mask[:, None, None, None, :], cache_score, -jnp.inf)
    fresh_score = jnp.where(fresh_mask, fresh_score, -jnp.inf)
    peak_score = jnp.maximum(
        jnp.max(cache_score, axis=-1, keepdims=True), jnp.max(fresh_score, axis=-1, keepdims=True)
    )
    cache_exp = jnp.exp(cache_score - peak_score)
    fresh_exp = jnp.exp(fresh_score - peak_score)
    total_exp = jnp.sum(cache_exp, axis=-1, keepdims=True) + jnp.sum(
        fresh_exp, axis=-1, keepdims=True
    )
    cache_prob = (cache_exp / total_exp).astype(jnp.bfloat16)
    fresh_prob = (fresh_exp / total_exp).astype(jnp.bfloat16)
    mixed = jnp.einsum(
        "rKgsc,rKcd->rsKgd", cache_prob, value_cache, preferred_element_type=jnp.float32
    )
    mixed = mixed + jnp.einsum(
        "rKgst,rtKd->rsKgd", fresh_prob, fresh_values, preferred_element_type=jnp.float32
    )
    return mixed.reshape(row_count, step_count, kv_heads * group_size * head_dim).astype(
        jnp.bfloat16
    )


def bit_swap(axis_total, bit):
    return [(i, i ^ bit) for i in range(axis_total)]


def depth_shift(axis_total, step):
    return [(i, (i + 8 * step) % axis_total) for i in range(axis_total)]


def take_half(blocks, which, axis):
    return lax.dynamic_index_in_dim(blocks, which, axis, keepdims=False)


def add_halves(kept, received):
    return (kept.astype(jnp.float32) + received.astype(jnp.float32)).astype(jnp.bfloat16)


def pick(blocks, which, axis):
    low = lax.index_in_dim(blocks, 0, axis, keepdims=False)
    high = lax.index_in_dim(blocks, 1, axis, keepdims=False)
    return jnp.where(which == 0, low, high)


def exchange_half(blocks, mine, axis, perm):
    received = lax.ppermute(pick(blocks, 1 - mine, axis), "fsdp", perm)
    return add_halves(pick(blocks, mine, axis), received)


def column_pieces(width, count):
    tiles = width // 128
    if width % 128 or tiles < count:
        return [(0, width)]
    edges = [128 * (tiles * i // count) for i in range(count + 1)]
    return [(edges[i], edges[i + 1]) for i in range(count)]


def summed_rows(pair_grad, pair_weighted, position, axis_total):
    depth = axis_total // 8
    my_z = position // 8
    my_y = (position // 4) % 2
    my_x = (position // 2) % 2
    my_core = position % 2
    row_total = pair_grad.shape[1]
    rows_chip = row_total // (axis_total // 2)
    finished = []
    for low, high in column_pieces(pair_weighted.shape[1], 5):
        partial = lax.dot_general(
            pair_grad,
            pair_weighted[:, low:high],
            (((0,), (0,)), ((), ())),
            preferred_element_type=jnp.float32,
        ).astype(jnp.bfloat16)
        width = high - low
        blocks = partial.reshape(depth, 2, 2, rows_chip, width)
        first = blocks[..., : width // 2]
        second = blocks[..., width // 2 :]
        first = exchange_half(first, my_x, 2, bit_swap(axis_total, 2))
        second = exchange_half(second, my_y, 1, bit_swap(axis_total, 4))
        first = exchange_half(first, my_y, 1, bit_swap(axis_total, 4))
        second = exchange_half(second, my_x, 1, bit_swap(axis_total, 2))
        both = jnp.concatenate([first, second], axis=-1)
        total = take_half(both, my_z, 0).astype(jnp.float32)
        for step in range(1, depth):
            outgoing = take_half(both, lax.rem(my_z + step, depth), 0)
            arrived = lax.ppermute(outgoing, "fsdp", depth_shift(axis_total, step))
            total = total + arrived.astype(jnp.float32)
        finished.append(total)
    chip_rows = jnp.concatenate(finished, axis=1)
    own_rows = chip_rows.shape[0] // 2
    halves = chip_rows.reshape(2, own_rows, chip_rows.shape[1])
    mine = take_half(halves, my_core, 0)
    theirs = lax.ppermute(
        take_half(halves, 1 - my_core, 0), "fsdp", bit_swap(axis_total, 1)
    )
    return jnp.where(
        my_core == 0,
        jnp.concatenate([mine, theirs], axis=1),
        jnp.concatenate([theirs, mine], axis=1),
    )


def per_device(
    hidden_in,
    out_grad,
    rewards,
    group_ids,
    weight,
    adam_m,
    adam_v,
    given_queries,
    given_keys,
    given_values,
    stored_keys,
    stored_values,
    cache_fill_length,
):
    seq_dev = rewards.shape[0]
    seq_total = seq_dev * lax.axis_size("fsdp")
    group_count = seq_total // GSIZE
    position = lax.axis_index("fsdp")
    labels = jnp.arange(group_count, dtype=jnp.int32)
    every_reward = lax.all_gather(rewards, "fsdp", axis=0, tiled=True)
    member = (group_ids[:, None] == labels[None, :]).astype(jnp.float32)
    group_mean = jnp.sum(member * every_reward[:, None], axis=0) / GSIZE
    spread_all = every_reward - jnp.sum(member * group_mean[None, :], axis=1)
    group_var = jnp.sum(member * (spread_all * spread_all)[:, None], axis=0) / (GSIZE - 1)
    group_std = jnp.sqrt(group_var)
    own_std = jnp.sum(member * group_std[None, :], axis=1)
    advantage = spread_all / jnp.maximum(own_std, std_floor)
    axis_total = lax.axis_size("fsdp")
    core = position % 2
    swap_core = bit_swap(axis_total, 1)
    token_count = hidden_in.shape[0]
    full_grad = lax.all_gather(out_grad, "tp", axis=1, tiled=True)
    half_width = hidden_in.shape[1] // 2
    low_half, high_half = hidden_in[:, :half_width], hidden_in[:, half_width:]
    other_grad = lax.ppermute(full_grad, "fsdp", swap_core)
    other_hidden = lax.ppermute(jnp.where(core == 0, high_half, low_half), "fsdp", swap_core)
    pair_grad = jnp.concatenate([full_grad, other_grad], axis=0)
    pair_hidden = jnp.concatenate([jnp.where(core == 0, low_half, high_half), other_hidden], axis=0)
    own_adv = lax.dynamic_slice_in_dim(advantage, position * seq_dev, seq_dev)
    other_adv = lax.dynamic_slice_in_dim(advantage, (position + 1 - 2 * core) * seq_dev, seq_dev)
    pair_adv = jnp.repeat(jnp.concatenate([own_adv, other_adv]), token_count // seq_dev)
    pair_weighted = (
        pair_hidden.astype(jnp.float32) * pair_adv[:, None] / seq_total
    ).astype(jnp.bfloat16)
    gradient = summed_rows(pair_grad, pair_weighted, position, axis_total)
    new_m = beta_one * adam_m + (1.0 - beta_one) * gradient
    new_v = beta_two * adam_v + (1.0 - beta_two) * gradient * gradient
    correct_one = 1.0 - beta_one**OPT_STEP
    correct_two = 1.0 - beta_two**OPT_STEP
    update = new_m / correct_one / (jnp.sqrt(new_v / correct_two) + adam_eps)
    new_weight = (
        weight.astype(jnp.float32) * (1.0 - learn_rate * decay_rate) - learn_rate * update
    ).astype(jnp.bfloat16)
    attn = attend_local(
        given_queries, given_keys, given_values, stored_keys, stored_values, cache_fill_length
    )
    row_count = attn.shape[0]
    step_count = attn.shape[1]
    attn_flat = attn.reshape(row_count * step_count, attn.shape[2])
    every_attn = lax.all_gather(attn_flat, "fsdp", axis=0, tiled=True)
    own_features = lax.dot_general(
        every_attn, new_weight, (((1,), (1,)), ((), ())), preferred_element_type=jnp.float32
    ).astype(jnp.bfloat16)
    partial_out = lax.all_to_all(
        own_features, "fsdp", split_axis=0, concat_axis=1, tiled=True
    ).astype(jnp.float32)
    summed = lax.psum_scatter(partial_out, "tp", scatter_dimension=1, tiled=True)
    layer_out = summed.reshape(row_count, step_count, summed.shape[1])
    return (new_weight, new_m, new_v, layer_out)


def solution(mesh):
    in_specs = (
        P("fsdp", "tp"),
        P("fsdp", "tp"),
        P("fsdp"),
        P(),
        P("fsdp", "tp"),
        P("fsdp", "tp"),
        P("fsdp", "tp"),
        P("fsdp", None, "tp"),
        P("fsdp", None, "tp"),
        P("fsdp", None, "tp"),
        P("fsdp", "tp", None, None),
        P("fsdp", "tp", None, None),
        P("fsdp"),
    )
    out_specs = (P("fsdp", "tp"), P("fsdp", "tp"), P("fsdp", "tp"), P("fsdp", None, "tp"))
    return jax.shard_map(
        per_device, mesh=mesh, in_specs=in_specs, out_specs=out_specs, check_vma=False
    )
```
